32 devices in a mesh: lat: 8 (over z, x), lon: 4 (over y, core).
Axes of the slice: x: 2, y: 2, z: 4, core: 2. Of those that a mesh axis runs over, the one named last changes fastest.
Arguments:
- state: float32 [4, 2, 192, 512], P(None, None, 'lat', 'lon'), may hold values from -6 to 6
- zonal_shift: int32 [2, 192], P(None, 'lat'), may hold values from -256 to 256, as said below
- zonal_cells: int32 [2, 192, 512], P(None, 'lat', 'lon'), may hold values from -2 to 2
- zonal_fraction: float32 [2, 192, 512], P(None, 'lat', 'lon'), may hold values from 0 to 1
- merid_cells: int32 [2, 192, 512], P(None, 'lat', 'lon'), may hold values from -1 to 1
- merid_fraction: float32 [2, 192, 512], P(None, 'lat', 'lon'), may hold values from 0 to 1
- coupling: float32 [2, 192, 512], P(None, 'lat', 'lon'), may hold values from 0.5 to 8
Outputs:
- advanced: float32 [4, 2, 192, 512], P(None, None, 'lat', 'lon')
The draws below stay inside these ranges and needn't reach their ends.
Inputs may be any that keep to these rules, and one draw needn't show every extreme that they name: `zonal_shift`: one whole-cell zonal displacement for each level and latitude row; bounded more tightly near the equator than near the poles.
All inputs are finite; a program needn't handle non-finite values.
Results may differ from the reference program's by a relative error of at most 0.00002.
Values sent between devices are 32-bit elements; how exact they have to be, the bound alone decides.
A program may use at most 128 MiB of HBM per device.

```python
import math
import jax
import jax.numpy as jnp
from jax import lax

FIELDS = 4
LEV = 2
SWEEPS = 4
NLAT = 192
NLON = 512


def draw_zonal_shift(key, part):
    rowids = jnp.arange(NLAT, dtype=jnp.int32)
    pole = jnp.minimum(rowids, NLAT - 1 - rowids)
    half = NLAT // 2
    span = NLON // 2
    reach = jnp.maximum(half - 1 - pole, 0)
    limit = 4 + (span - 4) * reach // max(half - 1, 1)
    limit = jnp.minimum(limit, span).astype(jnp.int32)
    lower = jnp.broadcast_to(-limit[None, :], (LEV, NLAT))
    upper = jnp.broadcast_to(limit[None, :] + 1, (LEV, NLAT))
    value = jax.random.randint(key, (LEV, NLAT), lower, upper, dtype=jnp.int32)
    levels = jnp.arange(LEV, dtype=jnp.int32)[:, None]
    edge = jnp.where(levels % 2 == 0, span, -span).astype(jnp.int32)
    value = jnp.where((rowids == 0)[None, :], edge, value)
    return value.astype(jnp.int32)


def set_ends(values, key, smallest, top_value):
    longest = values.shape.index(max(values.shape))
    spots = []
    for shift in (0, 1):
        where = [jax.random.randint(jax.random.fold_in(key, axis), (), 0, length) for axis, length in enumerate(values.shape)]
        where[longest] = (where[longest] + shift) % values.shape[longest]
        spots.append(tuple(where))
    return values.at[spots[0]].set(smallest).at[spots[1]].set(top_value)


def block_levels(stream_key, extent, split, low, high):
    gain, own = 1.0, jax.random.fold_in(stream_key, 6)
    for dim, parts in split:
        heights = jnp.exp(jax.random.uniform(jax.random.fold_in(own, dim), (parts,), jnp.float32, low / len(split), high / len(split)))
        gain = gain * jnp.repeat(heights, extent[dim] // parts).reshape([-1 if axis == dim else 1 for axis in range(len(extent))])
    return gain


def scatter_about(rng, shape, spread, most, cuts=(), kind=jnp.bfloat16):
    result = spread * jax.random.normal(rng, shape, jnp.float32)
    if cuts:
        result = result * block_levels(rng, shape, cuts, -0.22, 0.18)
    return jnp.clip(result, -most, most).astype(kind)


def setup_inputs(seed: int = 0) -> dict:
    keys = jax.random.split(jax.random.key(seed), 8)
    return {
        "state": scatter_about(keys[0], (FIELDS, LEV, NLAT, NLON), 1.0, 6.0, ((2, 8), (3, 4)), jnp.float32),
        "zonal_shift": draw_zonal_shift(jax.random.fold_in(keys[7], 71), 0),
        "zonal_cells": set_ends(jax.random.randint(keys[2], (LEV, NLAT, NLON), -2, 3), jax.random.fold_in(keys[2], 1), -2, 2).astype(jnp.int32),
        "zonal_fraction": jnp.clip(1.0 * jax.random.uniform(keys[3], (LEV, NLAT, NLON), jnp.float32) ** block_levels(keys[3], (LEV, NLAT, NLON), ((1, 8), (2, 4)), -0.2, 0.2), 0.0, 1.0),
        "merid_cells": set_ends(jax.random.randint(keys[4], (LEV, NLAT, NLON), -1, 2), jax.random.fold_in(keys[4], 1), -1, 1).astype(jnp.int32),
        "merid_fraction": jnp.clip(1.0 * jax.random.uniform(keys[5], (LEV, NLAT, NLON), jnp.float32) ** block_levels(keys[5], (LEV, NLAT, NLON), ((1, 8), (2, 4)), -0.2, 0.2), 0.0, 1.0),
        "coupling": jnp.clip(jnp.exp(math.log(8.0) - 2.7725887 * jax.random.uniform(keys[6], (LEV, NLAT, NLON), jnp.float32) ** block_levels(keys[6], (LEV, NLAT, NLON), ((1, 8), (2, 4)), -0.2, 0.2)), 0.5, 8.0),
    }


def cubic_weights(frac):
    return (-frac * (frac - 1.0) * (frac - 2.0) / 6.0,
            (frac + 1.0) * (frac - 1.0) * (frac - 2.0) / 2.0,
            -(frac + 1.0) * frac * (frac - 2.0) / 2.0,
            (frac + 1.0) * frac * (frac - 1.0) / 6.0)


def reference(state, zonal_shift, zonal_cells, zonal_fraction, merid_cells, merid_fraction, coupling):
    columns = jnp.arange(NLON, dtype=jnp.int32)
    rowids = jnp.arange(NLAT, dtype=jnp.int32)
    zonal_base = (columns[None, None, :] - zonal_shift[:, :, None] - zonal_cells).astype(jnp.int32)
    merid_base = (rowids[None, :, None] + 3 - merid_cells).astype(jnp.int32)
    zonal_w = cubic_weights(zonal_fraction)
    merid_w = cubic_weights(merid_fraction)

    def advance(field):
        zonal = jnp.zeros(field.shape, jnp.float32)
        for k in range(4):
            index = jnp.mod(zonal_base + (k - 1), NLON).astype(jnp.int32)
            zonal = zonal + zonal_w[k] * jnp.take_along_axis(field, index, axis=2)
        padded = jnp.pad(zonal, ((0, 0), (3, 3), (0, 0)))
        source = jnp.zeros(field.shape, jnp.float32)
        for k in range(4):
            index = (merid_base + (k - 1)).astype(jnp.int32)
            source = source + merid_w[k] * jnp.take_along_axis(padded, index, axis=1)
        phi = source
        for sweep in range(SWEEPS):
            rimmed = jnp.pad(phi, ((0, 0), (1, 1), (0, 0)))
            beside = rimmed[:, :-2, :] + rimmed[:, 2:, :]
            beside = beside + jnp.roll(phi, 1, axis=2) + jnp.roll(phi, -1, axis=2)
            phi = (source + coupling * beside) / (1.0 + 4.0 * coupling)
        return phi

    return lax.map(advance, state)
```

```python
import functools

import jax
import jax.numpy as jnp
from jax import lax
from jax.experimental import pallas as pl
from jax.experimental.pallas import tpu as pltpu
from jax.sharding import PartitionSpec as P

SWEEPS = 4
HALO = 8
MESH = pl.DeviceIdType.MESH


def cubic_weights(frac):
    return (
        -frac * (frac - 1.0) * (frac - 2.0) / 6.0,
        (frac + 1.0) * (frac - 1.0) * (frac - 2.0) / 2.0,
        -(frac + 1.0) * frac * (frac - 2.0) / 2.0,
        (frac + 1.0) * frac * (frac - 1.0) / 6.0,
    )


def take_lanes(value, index):
    return jnp.take_along_axis(value, index, axis=1, mode="promise_in_bounds")


def merid_parts(cells, frac):
    w = cubic_weights(frac)
    parts = []
    for offset in range(-2, 4):
        total = jnp.zeros_like(frac)
        for k in range(4):
            cell = k - 1 - offset
            if -1 <= cell <= 1:
                total = jnp.where(cells == float(cell), w[k], total)
        parts.append(total)
    return parts


def kernel(
    bands, sectors, state, shift, zcells, zfrac, mcells, mfrac, coup, out,
    ring, zmain, zwest, zeast, pmain, pwest, peast,
    y_send, y_recv, p_send, p_recv, h_send, h_recv, z_send, z_recv,
):
    fields, levels, rows, width = state.shape
    both = fields * levels
    halves = sectors // 2
    circle = sectors * width
    la, lo = lax.axis_index("lat"), lax.axis_index("lon")
    half = lo // 2
    core = lo - 2 * half
    partner = lo + 1 - 2 * core
    east = lax.rem(lo + 1, sectors)
    west = lax.rem(lo + sectors - 1, sectors)
    has_north, has_south = la > 0, la < bands - 1
    own = pl.ds(HALO, rows)

    barrier = pltpu.get_barrier_semaphore()

    def greet(to_la, to_lo):
        pl.semaphore_signal(barrier, inc=1, device_id=(to_la, to_lo), device_id_type=MESH)

    greet(la, east)
    greet(la, west)
    others = [2 * lax.rem(half + d, halves) + core for d in range(1, halves)]
    sources = [2 * lax.rem(half + halves - d, halves) + core for d in range(1, halves)]
    for other in others:
        greet(la, other)

    @pl.when(has_north)
    def _():
        for to_lo in (lo, east, west):
            greet(la - 1, to_lo)

    @pl.when(has_south)
    def _():
        for to_lo in (lo, east, west):
            greet(la + 1, to_lo)

    lane = lax.broadcasted_iota(jnp.int32, (rows, width), 1)
    group = lane // (2 * HALO)
    edge = ((lane & (HALO - 1)) + width - HALO // 2) & (width - 1)
    for at, ref in enumerate((mcells, mfrac, coup)):
        low = ref[0].astype(jnp.float32)
        high = ref[1].astype(jnp.float32)
        pmain[2 * at, own] = low
        pmain[2 * at + 1, own] = high
        packed = jnp.where((group & 1) == 0, take_lanes(low, edge), take_lanes(high, edge))
        pmain[6 + at, own] = packed
    ring[lo] = state[...]

    outer = jnp.logical_or(la == 0, la == bands - 1)

    @pl.when(outer)
    def _():
        pl.semaphore_wait(barrier, 1 + halves + 3)

    @pl.when(jnp.logical_not(outer))
    def _():
        pl.semaphore_wait(barrier, 1 + halves + 6)

    def remote(src, dst, send, recv, to_la, to_lo):
        return pltpu.make_async_remote_copy(
            src_ref=src, dst_ref=dst, send_sem=send, recv_sem=recv,
            device_id=(to_la, to_lo), device_id_type=MESH,
        )

    across, beside, relay = {}, {}, {}
    for f in range(fields):
        for d, other in enumerate(others):
            across[f, d] = remote(
                state.at[f], ring.at[lo, f], y_send.at[d, f], y_recv.at[d, f], la, other
            )
            across[f, d].start()
    for f in range(fields):
        beside[f] = remote(
            state.at[f], ring.at[lo, f], p_send.at[halves - 1, f], p_recv.at[halves - 1, f], la, partner
        )
        beside[f].start()

    def neighbours(main, to_west, to_east, first, count, send, recv):
        top, bottom = pl.ds(HALO, HALO), pl.ds(rows, HALO)
        before, after = pl.ds(0, HALO), pl.ds(rows + HALO, HALO)
        every = pl.ds(0, first + count)
        strip = pl.ds(first, count)
        none = None
        plan = [
            (main.at[every, top], main.at[every, after], la - 1, lo, has_north, has_south),
            (main.at[every, bottom], main.at[every, before], la + 1, lo, has_south, has_north),
            (main.at[strip, own], to_west.at[:, own], la, east, none, none),
            (main.at[strip, own], to_east.at[:, own], la, west, none, none),
            (main.at[strip, top], to_west.at[:, after], la - 1, east, has_north, has_south),
            (main.at[strip, top], to_east.at[:, after], la - 1, west, has_north, has_south),
            (main.at[strip, bottom], to_west.at[:, before], la + 1, east, has_south, has_north),
            (main.at[strip, bottom], to_east.at[:, before], la + 1, west, has_south, has_north),
        ]
        return [
            (remote(src, dst, send.at[i], recv.at[i], to_la, to_lo), goes, comes)
            for i, (src, dst, to_la, to_lo, goes, comes) in enumerate(plan)
        ]

    def guarded(condition, action):
        if condition is None:
            action()
        else:
            pl.when(condition)(action)

    params = neighbours(pmain, pwest, peast, 6, 3, h_send, h_recv)
    for copy, goes, _ in params:
        guarded(goes, copy.start)

    for condition, begin in ((la == 0, 0), (la == bands - 1, rows + HALO)):
        @pl.when(condition)
        def _(begin=begin):
            for ref in (zmain, zwest, zeast):
                ref[:, pl.ds(begin, HALO), :] = jnp.zeros((ref.shape[0], HALO, width), jnp.float32)

    square = (rows, rows)
    diagonal = lax.broadcasted_iota(jnp.int32, square, 0) == lax.broadcasted_iota(jnp.int32, square, 1)
    plans = []
    for l in range(levels):
        line = jnp.broadcast_to(shift[pl.ds(l, 1), :].astype(jnp.float32), square)
        moved = jnp.sum(jnp.where(diagonal, line, 0.0), axis=1, keepdims=True).astype(jnp.int32)
        base = lo * width - 3 - jnp.broadcast_to(moved, (rows, width))
        base = jnp.where(base < 0, base + circle, base)
        base = jnp.where(base >= circle, base - circle, base)
        hop = lax.shift_right_logical(base, width.bit_length() - 1)
        within = base & (width - 1)
        near = hop + jnp.where(lane < within, 1, 0)
        near = jnp.where(near >= sectors, near - sectors, near)
        far = near + 1
        far = jnp.where(far >= sectors, far - sectors, far)
        weights = cubic_weights(zfrac[l])
        cells = zcells[l]
        steps = []
        for k in range(4):
            place = lane + (k + 2) - cells
            steps.append((place >= width, (place + within) & (width - 1), weights[k]))
        plans.append((near, far, steps))

    def zonal_field(f):
        for l in range(levels):
            near, far, steps = plans[l]
            first = second = ring[0, f, l]
            for s in range(1, sectors):
                block = ring[s, f, l]
                first = jnp.where(near == s, block, first)
                second = jnp.where(far == s, block, second)
            total = None
            for beyond, index, weight in steps:
                value = jnp.where(beyond, take_lanes(second, index), take_lanes(first, index))
                total = weight * value if total is None else total + weight * value
            zmain[f * levels + l, own] = total
            picked = take_lanes(total, edge)
            at = f * levels + l
            if at == 0:
                zmain[both, own] = picked
            else:
                zmain[both, own] = jnp.where(group == at, picked, zmain[both, own])

    def pass_on(f):
        for d, source in enumerate(sources):
            across[f, d].wait_recv()
            relay[f, d] = remote(
                ring.at[source, f], ring.at[source, f], p_send.at[d, f], p_recv.at[d, f], la, partner
            )
            relay[f, d].start()

    pass_on(0)
    for f in range(fields):
        if f + 1 < fields:
            pass_on(f + 1)
        beside[f].wait_recv()
        for d in range(halves - 1):
            relay[f, d].wait_recv()
        zonal_field(f)

    zonal = neighbours(zmain, zwest, zeast, both, 1, z_send, z_recv)
    for copy, goes, _ in zonal:
        guarded(goes, copy.start)

    for copy, _, comes in params:
        guarded(comes, copy.wait_recv)
    tall = rows + HALO
    begin = HALO // 2
    body = pl.ds(begin, tall)
    wide = lax.broadcasted_iota(jnp.int32, (tall, width), 1)
    spot = wide & (2 * HALO - 1)
    line = lax.broadcasted_iota(jnp.int32, (tall, width), 0) + (la * rows - HALO // 2)
    inside = jnp.logical_and(line >= 0, line < bands * rows)

    def coefficients(cells, frac, coupling):
        inverse = jnp.where(inside, 1.0 / (1.0 + 4.0 * coupling), 0.0)
        linked = jnp.where(inside, coupling * inverse, 0.0)
        parts = [jnp.where(inside, part, 0.0) for part in merid_parts(cells, frac)]
        return parts, linked, inverse

    def joined(left, middle, right):
        return jnp.where(spot < HALO // 2, left, jnp.where(spot >= 3 * HALO // 2, right, middle))

    level_terms = [
        coefficients(pmain[l, body], pmain[2 + l, body], pmain[4 + l, body]) for l in range(levels)
    ]
    strip_terms = coefficients(
        *[joined(pwest[c, body], pmain[6 + c, body], peast[c, body]) for c in range(3)]
    )

    for copy, _, comes in zonal:
        guarded(comes, copy.wait_recv)

    def up_down(value):
        return pltpu.roll(value, 1, 0) + pltpu.roll(value, tall - 1, 0)

    parts, linked, inverse = strip_terms
    source = None
    for part, offset in zip(parts, range(-2, 4)):
        at = pl.ds(begin + offset, tall)
        term = part * joined(zwest[0, at], zmain[both, at], zeast[0, at])
        source = term if source is None else source + term
    scaled = source * inverse
    strips = [source]
    for sweep in range(SWEEPS - 1):
        last = strips[-1]
        around = up_down(last) + pltpu.roll(last, 1, 1) + pltpu.roll(last, width - 1, 1)
        strips.append(scaled + linked * around)

    first_lane, last_lane = wide == 0, wide == width - 1
    for at_field in range(both):
        parts, linked, inverse = level_terms[at_field % levels]
        source = None
        for part, offset in zip(parts, range(-2, 4)):
            term = part * zmain[at_field, pl.ds(begin + offset, tall)]
            source = term if source is None else source + term
        scaled = source * inverse
        ends = jnp.where(first_lane, HALO // 2 - 1, 3 * HALO // 2) + at_field * 2 * HALO
        phi = source
        for sweep in range(SWEEPS):
            beyond = take_lanes(strips[sweep], ends)
            before = jnp.where(first_lane, beyond, pltpu.roll(phi, 1, 1))
            after = jnp.where(last_lane, beyond, pltpu.roll(phi, width - 1, 1))
            phi = scaled + linked * (up_down(phi) + before + after)
        out[at_field // levels, at_field % levels] = phi[begin : begin + rows]

    for copy, goes, _ in params + zonal:
        guarded(goes, copy.wait_send)
    for f in range(fields):
        beside[f].wait_send()
        for d in range(halves - 1):
            across[f, d].wait_send()
            relay[f, d].wait_send()


def body(*args, bands, sectors):
    state = args[0]
    fields, levels, rows, width = state.shape
    both, halves = fields * levels, sectors // 2
    tall = rows + 2 * HALO
    f32 = jnp.float32
    spec = pl.BlockSpec(memory_space=pltpu.VMEM)
    pairs = pltpu.SemaphoreType.DMA((halves, fields))
    eight = pltpu.SemaphoreType.DMA((8,))
    return pl.pallas_call(
        functools.partial(kernel, bands, sectors),
        out_shape=jax.ShapeDtypeStruct(state.shape, f32),
        in_specs=[spec] * 7,
        out_specs=spec,
        scratch_shapes=[
            pltpu.VMEM((sectors,) + state.shape, f32),
            pltpu.VMEM((both + 1, tall, width), f32),
            pltpu.VMEM((1, tall, width), f32),
            pltpu.VMEM((1, tall, width), f32),
            pltpu.VMEM((9, tall, width), f32),
            pltpu.VMEM((3, tall, width), f32),
            pltpu.VMEM((3, tall, width), f32),
            pairs, pairs, pairs, pairs, eight, eight, eight, eight,
        ],
        compiler_params=pltpu.CompilerParams(
            collective_id=0, has_side_effects=True, vmem_limit_bytes=24 * 2**20
        ),
    )(*args)


def solution(mesh):
    in_specs = (
        P(None, None, "lat", "lon"),
        P(None, "lat"),
        P(None, "lat", "lon"),
        P(None, "lat", "lon"),
        P(None, "lat", "lon"),
        P(None, "lat", "lon"),
        P(None, "lat", "lon"),
    )
    out_specs = P(None, None, "lat", "lon")
    run = functools.partial(body, bands=mesh.shape["lat"], sectors=mesh.shape["lon"])
    return jax.shard_map(run, mesh=mesh, in_specs=in_specs, out_specs=out_specs, check_vma=False)
```

```python
import functools

import jax
import jax.numpy as jnp
from jax import lax
from jax.experimental import pallas as pl
from jax.experimental.pallas import tpu as pltpu
from jax.sharding import PartitionSpec as P

SWEEPS = 4
HALO = 8
MESH = pl.DeviceIdType.MESH


def cubic_weights(frac):
    return (
        -frac * (frac - 1.0) * (frac - 2.0) / 6.0,
        (frac + 1.0) * (frac - 1.0) * (frac - 2.0) / 2.0,
        -(frac + 1.0) * frac * (frac - 2.0) / 2.0,
        (frac + 1.0) * frac * (frac - 1.0) / 6.0,
    )


def take_lanes(value, index):
    return jnp.take_along_axis(value, index, axis=1, mode="promise_in_bounds")


def merid_parts(cells, frac):
    w = cubic_weights(frac)
    parts = []
    for offset in range(-2, 4):
        total = jnp.zeros_like(frac)
        for k in range(4):
            cell = k - 1 - offset
            if -1 <= cell <= 1:
                total = jnp.where(cells == float(cell), w[k], total)
        parts.append(total)
    return parts


def kernel(
    bands, sectors, state, shift_in, zcells_in, zfrac_in, mcells_in, mfrac, coup, out,
    ring, zmain, zwest, zeast, pmain, pwest, peast, shift, zcells, zfrac, mcells, loaded,
    y_send, y_recv, p_send, p_recv, h_send, h_recv, z_send, z_recv,
):
    fields, levels, rows, width = state.shape
    both = fields * levels
    halves = sectors // 2
    circle = sectors * width
    la, lo = lax.axis_index("lat"), lax.axis_index("lon")
    half = lo // 2
    core = lo - 2 * half
    partner = lo + 1 - 2 * core
    east = lax.rem(lo + 1, sectors)
    west = lax.rem(lo + sectors - 1, sectors)
    has_north, has_south = la > 0, la < bands - 1
    own = pl.ds(HALO, rows)

    barrier = pltpu.get_barrier_semaphore()

    def greet(to_la, to_lo):
        pl.semaphore_signal(barrier, inc=1, device_id=(to_la, to_lo), device_id_type=MESH)

    greet(la, east)
    greet(la, west)
    others = [2 * lax.rem(half + d, halves) + core for d in range(1, halves)]
    sources = [2 * lax.rem(half + halves - d, halves) + core for d in range(1, halves)]
    for other in others:
        greet(la, other)

    @pl.when(has_north)
    def _():
        for to_lo in (lo, east, west):
            greet(la - 1, to_lo)

    @pl.when(has_south)
    def _():
        for to_lo in (lo, east, west):
            greet(la + 1, to_lo)

    loads = [
        pltpu.make_async_copy(src, dst, loaded.at[i])
        for i, (src, dst) in enumerate((
            (state, ring.at[lo]),
            (mcells_in, mcells),
            (mfrac, pmain.at[pl.ds(levels, levels), own]),
            (coup, pmain.at[pl.ds(2 * levels, levels), own]),
            (shift_in, shift),
            (zcells_in, zcells),
            (zfrac_in, zfrac),
        ))
    ]
    for load in loads:
        load.start()

    for condition, begin in ((la == 0, 0), (la == bands - 1, rows + HALO)):
        @pl.when(condition)
        def _(begin=begin):
            for ref in (zmain, zwest, zeast):
                ref[:, pl.ds(begin, HALO), :] = jnp.zeros((ref.shape[0], HALO, width), jnp.float32)

    loads[0].wait()
    outer = jnp.logical_or(la == 0, la == bands - 1)

    @pl.when(outer)
    def _():
        pl.semaphore_wait(barrier, 1 + halves + 3)

    @pl.when(jnp.logical_not(outer))
    def _():
        pl.semaphore_wait(barrier, 1 + halves + 6)

    def remote(src, dst, send, recv, to_la, to_lo):
        return pltpu.make_async_remote_copy(
            src_ref=src, dst_ref=dst, send_sem=send, recv_sem=recv,
            device_id=(to_la, to_lo), device_id_type=MESH,
        )

    across, beside, relay = {}, {}, {}
    for f in range(fields):
        for d, other in enumerate(others):
            across[f, d] = remote(
                ring.at[lo, f], ring.at[lo, f], y_send.at[d, f], y_recv.at[d, f], la, other
            )
            across[f, d].start()
    for f in range(fields):
        beside[f] = remote(
            ring.at[lo, f], ring.at[lo, f], p_send.at[halves - 1, f], p_recv.at[halves - 1, f], la, partner
        )
        beside[f].start()

    def neighbours(main, to_west, to_east, first, count, send, recv):
        top, bottom = pl.ds(HALO, HALO), pl.ds(rows, HALO)
        before, after = pl.ds(0, HALO), pl.ds(rows + HALO, HALO)
        strip = pl.ds(first, count)
        none = None
        plan = [
            (main.at[strip, top], main.at[strip, after], la - 1, lo, has_north, has_south),
            (main.at[strip, bottom], main.at[strip, before], la + 1, lo, has_south, has_north),
            (main.at[strip, own], to_west.at[:, own], la, east, none, none),
            (main.at[strip, own], to_east.at[:, own], la, west, none, none),
            (main.at[strip, top], to_west.at[:, after], la - 1, east, has_north, has_south),
            (main.at[strip, top], to_east.at[:, after], la - 1, west, has_north, has_south),
            (main.at[strip, bottom], to_west.at[:, before], la + 1, east, has_south, has_north),
            (main.at[strip, bottom], to_east.at[:, before], la + 1, west, has_south, has_north),
        ]
        return [
            (remote(src, dst, send.at[i], recv.at[i], to_la, to_lo), goes, comes)
            for i, (src, dst, to_la, to_lo, goes, comes) in enumerate(plan)
        ]

    def straight(main, part, send, recv):
        top, bottom = pl.ds(HALO, HALO), pl.ds(rows, HALO)
        before, after = pl.ds(0, HALO), pl.ds(rows + HALO, HALO)
        return [
            (remote(main.at[part, top], main.at[part, after], send.at[0], recv.at[0], la - 1, lo),
             has_north, has_south),
            (remote(main.at[part, bottom], main.at[part, before], send.at[1], recv.at[1], la + 1, lo),
             has_south, has_north),
        ]

    def guarded(condition, action):
        if condition is None:
            action()
        else:
            pl.when(condition)(action)

    lane = lax.broadcasted_iota(jnp.int32, (rows, width), 1)
    group = lane // (2 * HALO)
    edge = ((lane & (HALO - 1)) + width - HALO // 2) & (width - 1)
    for load in loads[1:4]:
        load.wait()
    for l in range(levels):
        pmain[l, own] = mcells[l].astype(jnp.float32)
    for at in range(3):
        low, high = pmain[2 * at, own], pmain[2 * at + 1, own]
        packed = jnp.where((group & 1) == 0, take_lanes(low, edge), take_lanes(high, edge))
        pmain[6 + at, own] = packed

    params = straight(pmain, pl.ds(0, 6), h_send.at[pl.ds(8, 2)], h_recv.at[pl.ds(8, 2)])
    params += neighbours(pmain, pwest, peast, 6, 3, h_send, h_recv)
    for copy, goes, _ in params:
        guarded(goes, copy.start)

    for load in loads[4:]:
        load.wait()
    square = (rows, rows)
    diagonal = lax.broadcasted_iota(jnp.int32, square, 0) == lax.broadcasted_iota(jnp.int32, square, 1)
    plans = []
    for l in range(levels):
        line = jnp.broadcast_to(shift[pl.ds(l, 1), :].astype(jnp.float32), square)
        moved = jnp.sum(jnp.where(diagonal, line, 0.0), axis=1, keepdims=True).astype(jnp.int32)
        base = lo * width - 3 - jnp.broadcast_to(moved, (rows, width))
        base = jnp.where(base < 0, base + circle, base)
        base = jnp.where(base >= circle, base - circle, base)
        hop = lax.shift_right_logical(base, width.bit_length() - 1)
        within = base & (width - 1)
        near = hop + jnp.where(lane < within, 1, 0)
        near = jnp.where(near >= sectors, near - sectors, near)
        far = near + 1
        far = jnp.where(far >= sectors, far - sectors, far)
        weights = cubic_weights(zfrac[l])
        cells = zcells[l]
        steps = []
        for k in range(4):
            place = lane + (k + 2) - cells
            steps.append((place >= width, (place + within) & (width - 1), weights[k]))
        plans.append((near, far, steps))

    def zonal_field(f):
        for l in range(levels):
            near, far, steps = plans[l]
            first = second = ring[0, f, l]
            for s in range(1, sectors):
                block = ring[s, f, l]
                first = jnp.where(near == s, block, first)
                second = jnp.where(far == s, block, second)
            total = None
            for beyond, index, weight in steps:
                value = jnp.where(beyond, take_lanes(second, index), take_lanes(first, index))
                total = weight * value if total is None else total + weight * value
            zmain[f * levels + l, own] = total
            picked = take_lanes(total, edge)
            at = f * levels + l
            if at == 0:
                zmain[both, own] = picked
            else:
                zmain[both, own] = jnp.where(group == at, picked, zmain[both, own])

    def pass_on(f):
        for d, source in enumerate(sources):
            across[f, d].wait_recv()
            relay[f, d] = remote(
                ring.at[source, f], ring.at[source, f], p_send.at[d, f], p_recv.at[d, f], la, partner
            )
            relay[f, d].start()

    zonal = []
    pass_on(0)
    for f in range(fields):
        if f + 1 < fields:
            pass_on(f + 1)
        beside[f].wait_recv()
        for d in range(halves - 1):
            relay[f, d].wait_recv()
        zonal_field(f)
        if f + 1 == fields:
            last = neighbours(zmain, zwest, zeast, both, 1, z_send, z_recv)
            for copy, goes, _ in last:
                guarded(goes, copy.start)
            zonal += last
        pair = pl.ds(8 + 2 * f, 2)
        rowset = straight(zmain, pl.ds(f * levels, levels), z_send.at[pair], z_recv.at[pair])
        for copy, goes, _ in rowset:
            guarded(goes, copy.start)
        zonal += rowset

    for copy, _, comes in params:
        guarded(comes, copy.wait_recv)
    tall = rows + HALO
    begin = HALO // 2
    body = pl.ds(begin, tall)
    wide = lax.broadcasted_iota(jnp.int32, (tall, width), 1)
    spot = wide & (2 * HALO - 1)
    line = lax.broadcasted_iota(jnp.int32, (tall, width), 0) + (la * rows - HALO // 2)
    inside = jnp.logical_and(line >= 0, line < bands * rows)

    def coefficients(cells, frac, coupling):
        inverse = jnp.where(inside, 1.0 / (1.0 + 4.0 * coupling), 0.0)
        linked = jnp.where(inside, coupling * inverse, 0.0)
        parts = [jnp.where(inside, part, 0.0) for part in merid_parts(cells, frac)]
        return parts, linked, inverse

    def joined(left, middle, right):
        return jnp.where(spot < HALO // 2, left, jnp.where(spot >= 3 * HALO // 2, right, middle))

    level_terms = [
        coefficients(pmain[l, body], pmain[2 + l, body], pmain[4 + l, body]) for l in range(levels)
    ]
    strip_terms = coefficients(
        *[joined(pwest[c, body], pmain[6 + c, body], peast[c, body]) for c in range(3)]
    )

    for copy, _, comes in zonal:
        guarded(comes, copy.wait_recv)

    def up_down(value):
        return pltpu.roll(value, 1, 0) + pltpu.roll(value, tall - 1, 0)

    parts, linked, inverse = strip_terms
    source = None
    for part, offset in zip(parts, range(-2, 4)):
        at = pl.ds(begin + offset, tall)
        term = part * joined(zwest[0, at], zmain[both, at], zeast[0, at])
        source = term if source is None else source + term
    scaled = source * inverse
    strips = [source]
    for sweep in range(SWEEPS - 1):
        last = strips[-1]
        around = up_down(last) + pltpu.roll(last, 1, 1) + pltpu.roll(last, width - 1, 1)
        strips.append(scaled + linked * around)

    first_lane, last_lane = wide == 0, wide == width - 1
    for at_field in range(both):
        parts, linked, inverse = level_terms[at_field % levels]
        source = None
        for part, offset in zip(parts, range(-2, 4)):
            term = part * zmain[at_field, pl.ds(begin + offset, tall)]
            source = term if source is None else source + term
        scaled = source * inverse
        ends = jnp.where(first_lane, HALO // 2 - 1, 3 * HALO // 2) + at_field * 2 * HALO
        phi = source
        for sweep in range(SWEEPS):
            beyond = take_lanes(strips[sweep], ends)
            before = jnp.where(first_lane, beyond, pltpu.roll(phi, 1, 1))
            after = jnp.where(last_lane, beyond, pltpu.roll(phi, width - 1, 1))
            phi = scaled + linked * (up_down(phi) + before + after)
        out[at_field // levels, at_field % levels] = phi[begin : begin + rows]

    for copy, goes, _ in params + zonal:
        guarded(goes, copy.wait_send)
    for f in range(fields):
        beside[f].wait_send()
        for d in range(halves - 1):
            across[f, d].wait_send()
            relay[f, d].wait_send()


def body(*args, bands, sectors):
    state = args[0]
    fields, levels, rows, width = state.shape
    both, halves = fields * levels, sectors // 2
    tall = rows + 2 * HALO
    f32 = jnp.float32
    spec = pl.BlockSpec(memory_space=pltpu.VMEM)
    pairs = pltpu.SemaphoreType.DMA((halves, fields))
    ten = pltpu.SemaphoreType.DMA((10,))
    many = pltpu.SemaphoreType.DMA((8 + 2 * fields,))
    hbm = pl.BlockSpec(memory_space=pltpu.HBM)
    small = (levels, rows, width)
    return pl.pallas_call(
        functools.partial(kernel, bands, sectors),
        out_shape=jax.ShapeDtypeStruct(state.shape, f32),
        in_specs=[hbm] * 7,
        out_specs=spec,
        scratch_shapes=[
            pltpu.VMEM((sectors,) + state.shape, f32),
            pltpu.VMEM((both + 1, tall, width), f32),
            pltpu.VMEM((1, tall, width), f32),
            pltpu.VMEM((1, tall, width), f32),
            pltpu.VMEM((9, tall, width), f32),
            pltpu.VMEM((3, tall, width), f32),
            pltpu.VMEM((3, tall, width), f32),
            pltpu.VMEM((levels, rows), jnp.int32),
            pltpu.VMEM(small, jnp.int32),
            pltpu.VMEM(small, f32),
            pltpu.VMEM(small, jnp.int32),
            pltpu.SemaphoreType.DMA((7,)),
            pairs, pairs, pairs, pairs, ten, ten, many, many,
        ],
        compiler_params=pltpu.CompilerParams(
            collective_id=0, has_side_effects=True, vmem_limit_bytes=63 * 2**20
        ),
    )(*args)


def solution(mesh):
    in_specs = (
        P(None, None, "lat", "lon"),
        P(None, "lat"),
        P(None, "lat", "lon"),
        P(None, "lat", "lon"),
        P(None, "lat", "lon"),
        P(None, "lat", "lon"),
        P(None, "lat", "lon"),
    )
    out_specs = P(None, None, "lat", "lon")
    run = functools.partial(body, bands=mesh.shape["lat"], sectors=mesh.shape["lon"])
    return jax.shard_map(run, mesh=mesh, in_specs=in_specs, out_specs=out_specs, check_vma=False)
```

```python
import functools

import jax
import jax.numpy as jnp
from jax import lax
from jax.experimental import pallas as pl
from jax.experimental.pallas import tpu as pltpu
from jax.sharding import PartitionSpec as P

SWEEPS = 4
HALO = 8
MESH = pl.DeviceIdType.MESH


def cubic_weights(frac):
    return (
        -frac * (frac - 1.0) * (frac - 2.0) / 6.0,
        (frac + 1.0) * (frac - 1.0) * (frac - 2.0) / 2.0,
        -(frac + 1.0) * frac * (frac - 2.0) / 2.0,
        (frac + 1.0) * frac * (frac - 1.0) / 6.0,
    )


def take_lanes(value, index):
    return jnp.take_along_axis(value, index, axis=1, mode="promise_in_bounds")


def merid_parts(cells, frac):
    w = cubic_weights(frac)
    parts = []
    for offset in range(-2, 4):
        total = jnp.zeros_like(frac)
        for k in range(4):
            cell = k - 1 - offset
            if -1 <= cell <= 1:
                total = jnp.where(cells == float(cell), w[k], total)
        parts.append(total)
    return parts


def kernel(
    bands, sectors, state, shift_in, zcells_in, zfrac_in, mcells_in, mfrac, coup, out,
    ring, zmain, zwest, zeast, pmain, pwest, peast, shift, zcells, zfrac, mcells, loaded,
    y_send, y_recv, p_send, p_recv, h_send, h_recv, z_send, z_recv,
):
    fields, levels, rows, width = state.shape
    both = fields * levels
    halves = sectors // 2
    circle = sectors * width
    la, lo = lax.axis_index("lat"), lax.axis_index("lon")
    half = lo // 2
    core = lo - 2 * half
    partner = lo + 1 - 2 * core
    east = lax.rem(lo + 1, sectors)
    west = lax.rem(lo + sectors - 1, sectors)
    has_north, has_south = la > 0, la < bands - 1
    own = pl.ds(HALO, rows)

    barrier = pltpu.get_barrier_semaphore()

    def greet(to_la, to_lo):
        pl.semaphore_signal(barrier, inc=1, device_id=(to_la, to_lo), device_id_type=MESH)

    greet(la, east)
    greet(la, west)
    others = [2 * lax.rem(half + d, halves) + core for d in range(1, halves)]
    sources = [2 * lax.rem(half + halves - d, halves) + core for d in range(1, halves)]
    for other in others:
        greet(la, other)

    @pl.when(has_north)
    def _():
        for to_lo in (lo, east, west):
            greet(la - 1, to_lo)

    @pl.when(has_south)
    def _():
        for to_lo in (lo, east, west):
            greet(la + 1, to_lo)

    loads = [
        pltpu.make_async_copy(src, dst, loaded.at[i])
        for i, (src, dst) in enumerate((
            (state, ring.at[lo]),
            (mcells_in, mcells),
            (mfrac, pmain.at[pl.ds(levels, levels), own]),
            (coup, pmain.at[pl.ds(2 * levels, levels), own]),
            (shift_in, shift),
            (zcells_in, zcells),
            (zfrac_in, zfrac),
        ))
    ]
    for load in loads:
        load.start()

    for condition, begin in ((la == 0, 0), (la == bands - 1, rows + HALO)):
        @pl.when(condition)
        def _(begin=begin):
            for ref in (zmain, zwest, zeast):
                ref[:, pl.ds(begin, HALO), :] = jnp.zeros((ref.shape[0], HALO, width), jnp.float32)

    loads[0].wait()
    outer = jnp.logical_or(la == 0, la == bands - 1)

    @pl.when(outer)
    def _():
        pl.semaphore_wait(barrier, 1 + halves + 3)

    @pl.when(jnp.logical_not(outer))
    def _():
        pl.semaphore_wait(barrier, 1 + halves + 6)

    def remote(src, dst, send, recv, to_la, to_lo):
        return pltpu.make_async_remote_copy(
            src_ref=src, dst_ref=dst, send_sem=send, recv_sem=recv,
            device_id=(to_la, to_lo), device_id_type=MESH,
        )

    across, beside, relay = {}, {}, {}
    for f in range(fields):
        for d, other in enumerate(others):
            across[f, d] = remote(
                ring.at[lo, f], ring.at[lo, f], y_send.at[d, f], y_recv.at[d, f], la, other
            )
            across[f, d].start()
    for f in range(fields):
        beside[f] = remote(
            ring.at[lo, f], ring.at[lo, f], p_send.at[halves - 1, f], p_recv.at[halves - 1, f], la, partner
        )
        beside[f].start()

    def neighbours(main, to_west, to_east, first, count, send, recv):
        top, bottom = pl.ds(HALO, HALO), pl.ds(rows, HALO)
        before, after = pl.ds(0, HALO), pl.ds(rows + HALO, HALO)
        strip = pl.ds(first, count)
        none = None
        plan = [
            (main.at[strip, top], main.at[strip, after], la - 1, lo, has_north, has_south),
            (main.at[strip, bottom], main.at[strip, before], la + 1, lo, has_south, has_north),
            (main.at[strip, own], to_west.at[:, own], la, east, none, none),
            (main.at[strip, own], to_east.at[:, own], la, west, none, none),
            (main.at[strip, top], to_west.at[:, after], la - 1, east, has_north, has_south),
            (main.at[strip, top], to_east.at[:, after], la - 1, west, has_north, has_south),
            (main.at[strip, bottom], to_west.at[:, before], la + 1, east, has_south, has_north),
            (main.at[strip, bottom], to_east.at[:, before], la + 1, west, has_south, has_north),
        ]
        return [
            (remote(src, dst, send.at[i], recv.at[i], to_la, to_lo), goes, comes)
            for i, (src, dst, to_la, to_lo, goes, comes) in enumerate(plan)
        ]

    def straight(main, part, send, recv):
        top, bottom = pl.ds(HALO, HALO), pl.ds(rows, HALO)
        before, after = pl.ds(0, HALO), pl.ds(rows + HALO, HALO)
        return [
            (remote(main.at[part, top], main.at[part, after], send.at[0], recv.at[0], la - 1, lo),
             has_north, has_south),
            (remote(main.at[part, bottom], main.at[part, before], send.at[1], recv.at[1], la + 1, lo),
             has_south, has_north),
        ]

    def guarded(condition, action):
        if condition is None:
            action()
        else:
            pl.when(condition)(action)

    lane = lax.broadcasted_iota(jnp.int32, (rows, width), 1)
    group = lane // (2 * HALO)
    edge = ((lane & (HALO - 1)) + width - HALO // 2) & (width - 1)
    for load in loads[1:4]:
        load.wait()
    for l in range(levels):
        pmain[l, own] = mcells[l].astype(jnp.float32)
    for at in range(3):
        low, high = pmain[2 * at, own], pmain[2 * at + 1, own]
        packed = jnp.where((group & 1) == 0, take_lanes(low, edge), take_lanes(high, edge))
        pmain[6 + at, own] = packed

    params = straight(pmain, pl.ds(0, 6), h_send.at[pl.ds(8, 2)], h_recv.at[pl.ds(8, 2)])
    params += neighbours(pmain, pwest, peast, 6, 3, h_send, h_recv)
    for copy, goes, _ in params:
        guarded(goes, copy.start)

    for load in loads[4:]:
        load.wait()
    square = (rows, rows)
    diagonal = lax.broadcasted_iota(jnp.int32, square, 0) == lax.broadcasted_iota(jnp.int32, square, 1)
    plans = []
    for l in range(levels):
        line = jnp.broadcast_to(shift[pl.ds(l, 1), :].astype(jnp.float32), square)
        moved = jnp.sum(jnp.where(diagonal, line, 0.0), axis=1, keepdims=True).astype(jnp.int32)
        base = lo * width - 3 - jnp.broadcast_to(moved, (rows, width))
        base = jnp.where(base < 0, base + circle, base)
        base = jnp.where(base >= circle, base - circle, base)
        hop = lax.shift_right_logical(base, width.bit_length() - 1)
        within = base & (width - 1)
        near = hop + jnp.where(lane < within, 1, 0)
        near = jnp.where(near >= sectors, near - sectors, near)
        far = near + 1
        far = jnp.where(far >= sectors, far - sectors, far)
        weights = cubic_weights(zfrac[l])
        cells = zcells[l]
        steps = []
        for k in range(4):
            place = lane + (k + 2) - cells
            steps.append((place >= width, (place + within) & (width - 1), weights[k]))
        plans.append((near, far, steps))

    def zonal_field(f):
        for l in range(levels):
            near, far, steps = plans[l]
            first = second = ring[0, f, l]
            for s in range(1, sectors):
                block = ring[s, f, l]
                first = jnp.where(near == s, block, first)
                second = jnp.where(far == s, block, second)
            total = None
            for beyond, index, weight in steps:
                value = jnp.where(beyond, take_lanes(second, index), take_lanes(first, index))
                total = weight * value if total is None else total + weight * value
            zmain[f * levels + l, own] = total
            picked = take_lanes(total, edge)
            at = f * levels + l
            if at == 0:
                zmain[both, own] = picked
            else:
                zmain[both, own] = jnp.where(group == at, picked, zmain[both, own])

    def pass_on(f):
        for d, source in enumerate(sources):
            across[f, d].wait_recv()
            relay[f, d] = remote(
                ring.at[source, f], ring.at[source, f], p_send.at[d, f], p_recv.at[d, f], la, partner
            )
            relay[f, d].start()

    zonal = []
    pass_on(0)
    for f in range(fields):
        if f + 1 < fields:
            pass_on(f + 1)
        beside[f].wait_recv()
        for d in range(halves - 1):
            relay[f, d].wait_recv()
        zonal_field(f)
        if f + 1 == fields:
            last = neighbours(zmain, zwest, zeast, both, 1, z_send, z_recv)
            for copy, goes, _ in last:
                guarded(goes, copy.start)
            zonal += last
        pair = pl.ds(8 + 2 * f, 2)
        rowset = straight(zmain, pl.ds(f * levels, levels), z_send.at[pair], z_recv.at[pair])
        for copy, goes, _ in rowset:
            guarded(goes, copy.start)
        zonal += rowset

    for copy, _, comes in params:
        guarded(comes, copy.wait_recv)
    tall = rows + HALO
    begin = HALO // 2
    body = pl.ds(begin, tall)
    wide = lax.broadcasted_iota(jnp.int32, (tall, width), 1)
    spot = wide & (2 * HALO - 1)
    line = lax.broadcasted_iota(jnp.int32, (tall, width), 0) + (la * rows - HALO // 2)
    inside = jnp.logical_and(line >= 0, line < bands * rows)

    def coefficients(cells, frac, coupling):
        inverse = jnp.where(inside, 1.0 / (1.0 + 4.0 * coupling), 0.0)
        linked = jnp.where(inside, coupling * inverse, 0.0)
        parts = [jnp.where(inside, part, 0.0) for part in merid_parts(cells, frac)]
        return parts, linked, inverse

    def joined(left, middle, right):
        return jnp.where(spot < HALO // 2, left, jnp.where(spot >= 3 * HALO // 2, right, middle))

    level_terms = [
        coefficients(pmain[l, body], pmain[2 + l, body], pmain[4 + l, body]) for l in range(levels)
    ]
    strip_terms = coefficients(
        *[joined(pwest[c, body], pmain[6 + c, body], peast[c, body]) for c in range(3)]
    )

    for copy, _, comes in zonal:
        guarded(comes, copy.wait_recv)

    def up_down(value):
        return pltpu.roll(value, 1, 0) + pltpu.roll(value, tall - 1, 0)

    parts, linked, inverse = strip_terms
    source = None
    for part, offset in zip(parts, range(-2, 4)):
        at = pl.ds(begin + offset, tall)
        term = part * joined(zwest[0, at], zmain[both, at], zeast[0, at])
        source = term if source is None else source + term
    scaled = source * inverse
    strips = [source]
    for sweep in range(SWEEPS - 1):
        last = strips[-1]
        around = up_down(last) + pltpu.roll(last, 1, 1) + pltpu.roll(last, width - 1, 1)
        strips.append(scaled + linked * around)

    first_lane, last_lane = wide == 0, wide == width - 1
    for at_field in range(both):
        parts, linked, inverse = level_terms[at_field % levels]
        source = None
        for part, offset in zip(parts, range(-2, 4)):
            term = part * zmain[at_field, pl.ds(begin + offset, tall)]
            source = term if source is None else source + term
        scaled = source * inverse
        ends = jnp.where(first_lane, HALO // 2 - 1, 3 * HALO // 2) + at_field * 2 * HALO
        phi = source
        for sweep in range(SWEEPS):
            beyond = take_lanes(strips[sweep], ends)
            before = jnp.where(first_lane, beyond, pltpu.roll(phi, 1, 1))
            after = jnp.where(last_lane, beyond, pltpu.roll(phi, width - 1, 1))
            phi = scaled + linked * (up_down(phi) + before + after)
        out[at_field // levels, at_field % levels] = phi[begin : begin + rows]

    for copy, goes, _ in params + zonal:
        guarded(goes, copy.wait_send)
    for f in range(fields):
        beside[f].wait_send()
        for d in range(halves - 1):
            across[f, d].wait_send()
            relay[f, d].wait_send()


def body(*args, bands, sectors):
    state = args[0]
    fields, levels, rows, width = state.shape
    both, halves = fields * levels, sectors // 2
    tall = rows + 2 * HALO
    f32 = jnp.float32
    spec = pl.BlockSpec(memory_space=pltpu.VMEM)
    pairs = pltpu.SemaphoreType.DMA((halves, fields))
    ten = pltpu.SemaphoreType.DMA((10,))
    many = pltpu.SemaphoreType.DMA((8 + 2 * fields,))
    hbm = pl.BlockSpec(memory_space=pltpu.HBM)
    small = (levels, rows, width)
    return pl.pallas_call(
        functools.partial(kernel, bands, sectors),
        out_shape=jax.ShapeDtypeStruct(state.shape, f32),
        in_specs=[hbm] * 7,
        out_specs=spec,
        scratch_shapes=[
            pltpu.VMEM((sectors,) + state.shape, f32),
            pltpu.VMEM((both + 1, tall, width), f32),
            pltpu.VMEM((1, tall, width), f32),
            pltpu.VMEM((1, tall, width), f32),
            pltpu.VMEM((9, tall, width), f32),
            pltpu.VMEM((3, tall, width), f32),
            pltpu.VMEM((3, tall, width), f32),
            pltpu.VMEM((levels, rows), jnp.int32),
            pltpu.VMEM(small, jnp.int32),
            pltpu.VMEM(small, f32),
            pltpu.VMEM(small, jnp.int32),
            pltpu.SemaphoreType.DMA((7,)),
            pairs, pairs, pairs, pairs, ten, ten, many, many,
        ],
        compiler_params=pltpu.CompilerParams(
            collective_id=0, has_side_effects=True, vmem_limit_bytes=24 * 2**20
        ),
    )(*[pltpu.with_memory_space_constraint(x, pltpu.HBM) for x in args])


def solution(mesh):
    in_specs = (
        P(None, None, "lat", "lon"),
        P(None, "lat"),
        P(None, "lat", "lon"),
        P(None, "lat", "lon"),
        P(None, "lat", "lon"),
        P(None, "lat", "lon"),
        P(None, "lat", "lon"),
    )
    out_specs = P(None, None, "lat", "lon")
    run = functools.partial(body, bands=mesh.shape["lat"], sectors=mesh.shape["lon"])
    return jax.shard_map(run, mesh=mesh, in_specs=in_specs, out_specs=out_specs, check_vma=False)
```

```python
import functools

import jax
import jax.numpy as jnp
from jax import lax
from jax.experimental import pallas as pl
from jax.experimental.pallas import tpu as pltpu
from jax.sharding import PartitionSpec as P

SWEEPS = 4
HALO = 8
MESH = pl.DeviceIdType.MESH


def cubic_weights(frac):
    return (
        -frac * (frac - 1.0) * (frac - 2.0) / 6.0,
        (frac + 1.0) * (frac - 1.0) * (frac - 2.0) / 2.0,
        -(frac + 1.0) * frac * (frac - 2.0) / 2.0,
        (frac + 1.0) * frac * (frac - 1.0) / 6.0,
    )


def take_lanes(value, index):
    return jnp.take_along_axis(value, index, axis=1, mode="promise_in_bounds")


def merid_parts(cells, frac):
    w = cubic_weights(frac)
    parts = []
    for offset in range(-2, 4):
        total = jnp.zeros_like(frac)
        for k in range(4):
            cell = k - 1 - offset
            if -1 <= cell <= 1:
                total = jnp.where(cells == float(cell), w[k], total)
        parts.append(total)
    return parts


def kernel(
    bands, sectors, state, shift_in, zcells_in, zfrac_in, mcells_in, mfrac, coup, out,
    ring, zmain, zwest, zeast, pmain, pwest, peast, shift, zcells, zfrac, mcells, loaded,
    y_send, y_recv, p_send, p_recv, h_send, h_recv, z_send, z_recv,
):
    fields, levels, rows, width = state.shape
    both = fields * levels
    halves = sectors // 2
    circle = sectors * width
    la, lo = lax.axis_index("lat"), lax.axis_index("lon")
    half = lo // 2
    core = lo - 2 * half
    partner = lo + 1 - 2 * core
    east = lax.rem(lo + 1, sectors)
    west = lax.rem(lo + sectors - 1, sectors)
    has_north, has_south = la > 0, la < bands - 1
    own = pl.ds(HALO, rows)

    barrier = pltpu.get_barrier_semaphore()

    def greet(to_la, to_lo):
        pl.semaphore_signal(barrier, inc=1, device_id=(to_la, to_lo), device_id_type=MESH)

    greet(la, east)
    greet(la, west)
    others = [2 * lax.rem(half + d, halves) + core for d in range(1, halves)]
    sources = [2 * lax.rem(half + halves - d, halves) + core for d in range(1, halves)]
    for other in others:
        greet(la, other)

    @pl.when(has_north)
    def _():
        for to_lo in (lo, east, west):
            greet(la - 1, to_lo)

    @pl.when(has_south)
    def _():
        for to_lo in (lo, east, west):
            greet(la + 1, to_lo)

    loads = [
        pltpu.make_async_copy(src, dst, loaded.at[i])
        for i, (src, dst) in enumerate((
            (state, ring.at[lo]),
            (mcells_in, mcells),
            (mfrac, pmain.at[pl.ds(levels, levels), own]),
            (coup, pmain.at[pl.ds(2 * levels, levels), own]),
            (shift_in, shift),
            (zcells_in, zcells),
            (zfrac_in, zfrac),
        ))
    ]
    for load in loads:
        load.start()

    for condition, begin in ((la == 0, 0), (la == bands - 1, rows + HALO)):
        @pl.when(condition)
        def _(begin=begin):
            for ref in (zmain, zwest, zeast):
                ref[:, pl.ds(begin, HALO), :] = jnp.zeros((ref.shape[0], HALO, width), jnp.float32)

    loads[0].wait()
    outer = jnp.logical_or(la == 0, la == bands - 1)

    @pl.when(outer)
    def _():
        pl.semaphore_wait(barrier, 1 + halves + 3)

    @pl.when(jnp.logical_not(outer))
    def _():
        pl.semaphore_wait(barrier, 1 + halves + 6)

    def remote(src, dst, send, recv, to_la, to_lo):
        return pltpu.make_async_remote_copy(
            src_ref=src, dst_ref=dst, send_sem=send, recv_sem=recv,
            device_id=(to_la, to_lo), device_id_type=MESH,
        )

    across, beside, relay = {}, {}, {}
    for f in range(fields):
        for d, other in enumerate(others):
            across[f, d] = remote(
                ring.at[lo, f], ring.at[lo, f], y_send.at[d, f], y_recv.at[d, f], la, other
            )
            across[f, d].start()
    for f in range(fields):
        beside[f] = remote(
            ring.at[lo, f], ring.at[lo, f], p_send.at[halves - 1, f], p_recv.at[halves - 1, f], la, partner
        )
        beside[f].start()

    def neighbours(main, to_west, to_east, first, count, send, recv):
        top, bottom = pl.ds(HALO, HALO), pl.ds(rows, HALO)
        before, after = pl.ds(0, HALO), pl.ds(rows + HALO, HALO)
        strip = pl.ds(first, count)
        none = None
        plan = [
            (main.at[strip, top], main.at[strip, after], la - 1, lo, has_north, has_south),
            (main.at[strip, bottom], main.at[strip, before], la + 1, lo, has_south, has_north),
            (main.at[strip, own], to_west.at[:, own], la, east, none, none),
            (main.at[strip, own], to_east.at[:, own], la, west, none, none),
            (main.at[strip, top], to_west.at[:, after], la - 1, east, has_north, has_south),
            (main.at[strip, top], to_east.at[:, after], la - 1, west, has_north, has_south),
            (main.at[strip, bottom], to_west.at[:, before], la + 1, east, has_south, has_north),
            (main.at[strip, bottom], to_east.at[:, before], la + 1, west, has_south, has_north),
        ]
        return [
            (remote(src, dst, send.at[i], recv.at[i], to_la, to_lo), goes, comes)
            for i, (src, dst, to_la, to_lo, goes, comes) in enumerate(plan)
        ]

    def straight(main, part, send, recv):
        top, bottom = pl.ds(HALO, HALO), pl.ds(rows, HALO)
        before, after = pl.ds(0, HALO), pl.ds(rows + HALO, HALO)
        return [
            (remote(main.at[part, top], main.at[part, after], send.at[0], recv.at[0], la - 1, lo),
             has_north, has_south),
            (remote(main.at[part, bottom], main.at[part, before], send.at[1], recv.at[1], la + 1, lo),
             has_south, has_north),
        ]

    def guarded(condition, action):
        if condition is None:
            action()
        else:
            pl.when(condition)(action)

    lane = lax.broadcasted_iota(jnp.int32, (rows, width), 1)
    group = lane // (2 * HALO)
    edge = ((lane & (HALO - 1)) + width - HALO // 2) & (width - 1)
    for load in loads[1:4]:
        load.wait()
    for l in range(levels):
        pmain[l, own] = mcells[l].astype(jnp.float32)
    for at in range(3):
        low, high = pmain[2 * at, own], pmain[2 * at + 1, own]
        picked = jnp.where((group & 1) == 0, take_lanes(low, edge), take_lanes(high, edge))
        packed = picked if at == 0 else jnp.where((group // 2) == at, picked, packed)
    pmain[6, own] = packed

    params = straight(pmain, pl.ds(0, 6), h_send.at[pl.ds(8, 2)], h_recv.at[pl.ds(8, 2)])
    params += neighbours(pmain, pwest, peast, 6, 1, h_send, h_recv)
    for copy, goes, _ in params:
        guarded(goes, copy.start)

    for load in loads[4:]:
        load.wait()
    square = (rows, rows)
    diagonal = lax.broadcasted_iota(jnp.int32, square, 0) == lax.broadcasted_iota(jnp.int32, square, 1)
    plans = []
    for l in range(levels):
        line = jnp.broadcast_to(shift[pl.ds(l, 1), :].astype(jnp.float32), square)
        moved = jnp.sum(jnp.where(diagonal, line, 0.0), axis=1, keepdims=True).astype(jnp.int32)
        base = lo * width - 3 - jnp.broadcast_to(moved, (rows, width))
        base = jnp.where(base < 0, base + circle, base)
        base = jnp.where(base >= circle, base - circle, base)
        hop = lax.shift_right_logical(base, width.bit_length() - 1)
        within = base & (width - 1)
        near = hop + jnp.where(lane < within, 1, 0)
        near = jnp.where(near >= sectors, near - sectors, near)
        far = near + 1
        far = jnp.where(far >= sectors, far - sectors, far)
        weights = cubic_weights(zfrac[l])
        cells = zcells[l]
        steps = []
        for k in range(4):
            place = lane + (k + 2) - cells
            steps.append((place >= width, (place + within) & (width - 1), weights[k]))
        plans.append((near, far, steps))

    def zonal_field(f):
        for l in range(levels):
            near, far, steps = plans[l]
            first = second = ring[0, f, l]
            for s in range(1, sectors):
                block = ring[s, f, l]
                first = jnp.where(near == s, block, first)
                second = jnp.where(far == s, block, second)
            total = None
            for beyond, index, weight in steps:
                value = jnp.where(beyond, take_lanes(second, index), take_lanes(first, index))
                total = weight * value if total is None else total + weight * value
            zmain[f * levels + l, own] = total
            picked = take_lanes(total, edge)
            at = f * levels + l
            if at == 0:
                zmain[both, own] = picked
            else:
                zmain[both, own] = jnp.where(group == at, picked, zmain[both, own])

    def pass_on(f):
        for d, source in enumerate(sources):
            across[f, d].wait_recv()
            relay[f, d] = remote(
                ring.at[source, f], ring.at[source, f], p_send.at[d, f], p_recv.at[d, f], la, partner
            )
            relay[f, d].start()

    zonal = []
    pass_on(0)
    for f in range(fields):
        if f + 1 < fields:
            pass_on(f + 1)
        beside[f].wait_recv()
        for d in range(halves - 1):
            relay[f, d].wait_recv()
        zonal_field(f)
        if f + 1 == fields:
            last = neighbours(zmain, zwest, zeast, both, 1, z_send, z_recv)
            for copy, goes, _ in last:
                guarded(goes, copy.start)
            zonal += last
        pair = pl.ds(8 + 2 * f, 2)
        rowset = straight(zmain, pl.ds(f * levels, levels), z_send.at[pair], z_recv.at[pair])
        for copy, goes, _ in rowset:
            guarded(goes, copy.start)
        zonal += rowset

    for copy, _, comes in params:
        guarded(comes, copy.wait_recv)
    tall = rows + HALO
    begin = HALO // 2
    body = pl.ds(begin, tall)
    wide = lax.broadcasted_iota(jnp.int32, (tall, width), 1)
    spot = wide & (2 * HALO - 1)
    line = lax.broadcasted_iota(jnp.int32, (tall, width), 0) + (la * rows - HALO // 2)
    inside = jnp.logical_and(line >= 0, line < bands * rows)

    def coefficients(cells, frac, coupling):
        inverse = jnp.where(inside, 1.0 / (1.0 + 4.0 * coupling), 0.0)
        linked = jnp.where(inside, coupling * inverse, 0.0)
        parts = [jnp.where(inside, part, 0.0) for part in merid_parts(cells, frac)]
        return parts, linked, inverse

    def joined(left, middle, right):
        return jnp.where(spot < HALO // 2, left, jnp.where(spot >= 3 * HALO // 2, right, middle))

    level_terms = [
        coefficients(pmain[l, body], pmain[2 + l, body], pmain[4 + l, body]) for l in range(levels)
    ]
    edges = joined(pwest[0, body], pmain[6, body], peast[0, body])
    pair = wide & (4 * HALO - 1)
    strip_terms = coefficients(*[take_lanes(edges, pair + 4 * HALO * c) for c in range(3)])

    for copy, _, comes in zonal:
        guarded(comes, copy.wait_recv)

    def up_down(value):
        return pltpu.roll(value, 1, 0) + pltpu.roll(value, tall - 1, 0)

    parts, linked, inverse = strip_terms
    source = None
    for part, offset in zip(parts, range(-2, 4)):
        at = pl.ds(begin + offset, tall)
        term = part * joined(zwest[0, at], zmain[both, at], zeast[0, at])
        source = term if source is None else source + term
    scaled = source * inverse
    strips = [source]
    for sweep in range(SWEEPS - 1):
        last = strips[-1]
        around = up_down(last) + pltpu.roll(last, 1, 1) + pltpu.roll(last, width - 1, 1)
        strips.append(scaled + linked * around)

    first_lane, last_lane = wide == 0, wide == width - 1
    for at_field in range(both):
        parts, linked, inverse = level_terms[at_field % levels]
        source = None
        for part, offset in zip(parts, range(-2, 4)):
            term = part * zmain[at_field, pl.ds(begin + offset, tall)]
            source = term if source is None else source + term
        scaled = source * inverse
        ends = jnp.where(first_lane, HALO // 2 - 1, 3 * HALO // 2) + at_field * 2 * HALO
        phi = source
        for sweep in range(SWEEPS):
            beyond = take_lanes(strips[sweep], ends)
            before = jnp.where(first_lane, beyond, pltpu.roll(phi, 1, 1))
            after = jnp.where(last_lane, beyond, pltpu.roll(phi, width - 1, 1))
            phi = scaled + linked * (up_down(phi) + before + after)
        out[at_field // levels, at_field % levels] = phi[begin : begin + rows]

    for copy, goes, _ in params + zonal:
        guarded(goes, copy.wait_send)
    for f in range(fields):
        beside[f].wait_send()
        for d in range(halves - 1):
            across[f, d].wait_send()
            relay[f, d].wait_send()


def body(*args, bands, sectors):
    state = args[0]
    fields, levels, rows, width = state.shape
    both, halves = fields * levels, sectors // 2
    tall = rows + 2 * HALO
    f32 = jnp.float32
    spec = pl.BlockSpec(memory_space=pltpu.VMEM)
    pairs = pltpu.SemaphoreType.DMA((halves, fields))
    ten = pltpu.SemaphoreType.DMA((10,))
    many = pltpu.SemaphoreType.DMA((8 + 2 * fields,))
    hbm = pl.BlockSpec(memory_space=pltpu.HBM)
    small = (levels, rows, width)
    return pl.pallas_call(
        functools.partial(kernel, bands, sectors),
        out_shape=jax.ShapeDtypeStruct(state.shape, f32),
        in_specs=[hbm] * 7,
        out_specs=spec,
        scratch_shapes=[
            pltpu.VMEM((sectors,) + state.shape, f32),
            pltpu.VMEM((both + 1, tall, width), f32),
            pltpu.VMEM((1, tall, width), f32),
            pltpu.VMEM((1, tall, width), f32),
            pltpu.VMEM((7, tall, width), f32),
            pltpu.VMEM((1, tall, width), f32),
            pltpu.VMEM((1, tall, width), f32),
            pltpu.VMEM((levels, rows), jnp.int32),
            pltpu.VMEM(small, jnp.int32),
            pltpu.VMEM(small, f32),
            pltpu.VMEM(small, jnp.int32),
            pltpu.SemaphoreType.DMA((7,)),
            pairs, pairs, pairs, pairs, ten, ten, many, many,
        ],
        compiler_params=pltpu.CompilerParams(
            collective_id=0, has_side_effects=True, vmem_limit_bytes=24 * 2**20
        ),
    )(*[pltpu.with_memory_space_constraint(x, pltpu.HBM) for x in args])


def solution(mesh):
    in_specs = (
        P(None, None, "lat", "lon"),
        P(None, "lat"),
        P(None, "lat", "lon"),
        P(None, "lat", "lon"),
        P(None, "lat", "lon"),
        P(None, "lat", "lon"),
        P(None, "lat", "lon"),
    )
    out_specs = P(None, None, "lat", "lon")
    run = functools.partial(body, bands=mesh.shape["lat"], sectors=mesh.shape["lon"])
    return jax.shard_map(run, mesh=mesh, in_specs=in_specs, out_specs=out_specs, check_vma=False)
```

```python
import functools

import jax
import jax.numpy as jnp
from jax import lax
from jax.experimental import pallas as pl
from jax.experimental.pallas import tpu as pltpu
from jax.sharding import PartitionSpec as P

SWEEPS = 4
HALO = 8
MESH = pl.DeviceIdType.MESH


def cubic_weights(frac):
    return (
        -frac * (frac - 1.0) * (frac - 2.0) / 6.0,
        (frac + 1.0) * (frac - 1.0) * (frac - 2.0) / 2.0,
        -(frac + 1.0) * frac * (frac - 2.0) / 2.0,
        (frac + 1.0) * frac * (frac - 1.0) / 6.0,
    )


def take_lanes(value, index):
    return jnp.take_along_axis(value, index, axis=1, mode="promise_in_bounds")


def merid_parts(cells, frac):
    w = cubic_weights(frac)
    parts = []
    for offset in range(-2, 4):
        total = jnp.zeros_like(frac)
        for k in range(4):
            cell = k - 1 - offset
            if -1 <= cell <= 1:
                total = jnp.where(cells == float(cell), w[k], total)
        parts.append(total)
    return parts


def kernel(
    bands, sectors, state, shift_in, zcells_in, zfrac_in, mcells_in, mfrac, coup, out,
    ring, zmain, zwest, zeast, pmain, pwest, peast, shift, zcells, zfrac, mcells, loaded,
    y_send, y_recv, p_send, p_recv, h_send, h_recv, z_send, z_recv,
):
    fields, levels, rows, width = state.shape
    both = fields * levels
    halves = sectors // 2
    circle = sectors * width
    la, lo = lax.axis_index("lat"), lax.axis_index("lon")
    half = lo // 2
    core = lo - 2 * half
    partner = lo + 1 - 2 * core
    east = lax.rem(lo + 1, sectors)
    west = lax.rem(lo + sectors - 1, sectors)
    has_north, has_south = la > 0, la < bands - 1
    own = pl.ds(HALO, rows)

    barrier = pltpu.get_barrier_semaphore()

    def greet(to_la, to_lo):
        pl.semaphore_signal(barrier, inc=1, device_id=(to_la, to_lo), device_id_type=MESH)

    greet(la, east)
    greet(la, west)
    others = [2 * lax.rem(half + d, halves) + core for d in range(1, halves)]
    sources = [2 * lax.rem(half + halves - d, halves) + core for d in range(1, halves)]
    for other in others:
        greet(la, other)

    @pl.when(has_north)
    def _():
        for to_lo in (lo, east, west):
            greet(la - 1, to_lo)

    @pl.when(has_south)
    def _():
        for to_lo in (lo, east, west):
            greet(la + 1, to_lo)

    loads = [
        pltpu.make_async_copy(src, dst, loaded.at[i])
        for i, (src, dst) in enumerate((
            (state, ring.at[lo]),
            (mcells_in, mcells),
            (mfrac, pmain.at[pl.ds(levels, levels), own]),
            (coup, pmain.at[pl.ds(2 * levels, levels), own]),
            (shift_in, shift),
            (zcells_in, zcells),
            (zfrac_in, zfrac),
        ))
    ]
    for load in loads:
        load.start()

    for condition, begin in ((la == 0, 0), (la == bands - 1, rows + HALO)):
        @pl.when(condition)
        def _(begin=begin):
            for ref in (zmain, zwest, zeast):
                ref[:, pl.ds(begin, HALO), :] = jnp.zeros((ref.shape[0], HALO, width), jnp.float32)

    loads[0].wait()
    outer = jnp.logical_or(la == 0, la == bands - 1)

    @pl.when(outer)
    def _():
        pl.semaphore_wait(barrier, 1 + halves + 3)

    @pl.when(jnp.logical_not(outer))
    def _():
        pl.semaphore_wait(barrier, 1 + halves + 6)

    def remote(src, dst, send, recv, to_la, to_lo):
        return pltpu.make_async_remote_copy(
            src_ref=src, dst_ref=dst, send_sem=send, recv_sem=recv,
            device_id=(to_la, to_lo), device_id_type=MESH,
        )

    across, beside, relay = {}, {}, {}
    for f in range(fields):
        for d, other in enumerate(others):
            across[f, d] = remote(
                ring.at[lo, f], ring.at[lo, f], y_send.at[d, f], y_recv.at[d, f], la, other
            )
            across[f, d].start()
    for f in range(fields):
        beside[f] = remote(
            ring.at[lo, f], ring.at[lo, f], p_send.at[halves - 1, f], p_recv.at[halves - 1, f], la, partner
        )
        beside[f].start()

    def neighbours(main, to_west, to_east, first, count, send, recv):
        top, bottom = pl.ds(HALO, HALO), pl.ds(rows, HALO)
        before, after = pl.ds(0, HALO), pl.ds(rows + HALO, HALO)
        strip = pl.ds(first, count)
        none = None
        plan = [
            (main.at[strip, top], main.at[strip, after], la - 1, lo, has_north, has_south),
            (main.at[strip, bottom], main.at[strip, before], la + 1, lo, has_south, has_north),
            (main.at[strip, own], to_west.at[:, own], la, east, none, none),
            (main.at[strip, own], to_east.at[:, own], la, west, none, none),
            (main.at[strip, top], to_west.at[:, after], la - 1, east, has_north, has_south),
            (main.at[strip, top], to_east.at[:, after], la - 1, west, has_north, has_south),
            (main.at[strip, bottom], to_west.at[:, before], la + 1, east, has_south, has_north),
            (main.at[strip, bottom], to_east.at[:, before], la + 1, west, has_south, has_north),
        ]
        return [
            (remote(src, dst, send.at[i], recv.at[i], to_la, to_lo), goes, comes)
            for i, (src, dst, to_la, to_lo, goes, comes) in enumerate(plan)
        ]

    def straight(main, part, send, recv):
        top, bottom = pl.ds(HALO, HALO), pl.ds(rows, HALO)
        before, after = pl.ds(0, HALO), pl.ds(rows + HALO, HALO)
        return [
            (remote(main.at[part, top], main.at[part, after], send.at[0], recv.at[0], la - 1, lo),
             has_north, has_south),
            (remote(main.at[part, bottom], main.at[part, before], send.at[1], recv.at[1], la + 1, lo),
             has_south, has_north),
        ]

    def guarded(condition, action):
        if condition is None:
            action()
        else:
            pl.when(condition)(action)

    lane = lax.broadcasted_iota(jnp.int32, (rows, width), 1)
    group = lane // (2 * HALO)
    edge = ((lane & (HALO - 1)) + width - HALO // 2) & (width - 1)
    for load in loads[1:4]:
        load.wait()
    for l in range(levels):
        pmain[l, own] = mcells[l].astype(jnp.float32)
    for at in range(3):
        low, high = pmain[2 * at, own], pmain[2 * at + 1, own]
        picked = jnp.where((group & 1) == 0, take_lanes(low, edge), take_lanes(high, edge))
        packed = picked if at == 0 else jnp.where((group // 2) == at, picked, packed)
    pmain[6, own] = packed

    params = straight(pmain, pl.ds(0, 6), h_send.at[pl.ds(8, 2)], h_recv.at[pl.ds(8, 2)])
    params += neighbours(pmain, pwest, peast, 6, 1, h_send, h_recv)
    for copy, goes, _ in params:
        guarded(goes, copy.start)

    for load in loads[4:]:
        load.wait()
    square = (rows, rows)
    diagonal = lax.broadcasted_iota(jnp.int32, square, 0) == lax.broadcasted_iota(jnp.int32, square, 1)
    plans = []
    for l in range(levels):
        line = jnp.broadcast_to(shift[pl.ds(l, 1), :].astype(jnp.float32), square)
        moved = jnp.sum(jnp.where(diagonal, line, 0.0), axis=1, keepdims=True).astype(jnp.int32)
        base = lo * width - 3 - jnp.broadcast_to(moved, (rows, width))
        base = jnp.where(base < 0, base + circle, base)
        base = jnp.where(base >= circle, base - circle, base)
        hop = lax.shift_right_logical(base, width.bit_length() - 1)
        within = base & (width - 1)
        near = hop + jnp.where(lane < within, 1, 0)
        near = jnp.where(near >= sectors, near - sectors, near)
        far = near + 1
        far = jnp.where(far >= sectors, far - sectors, far)
        weights = cubic_weights(zfrac[l])
        cells = zcells[l]
        steps = []
        for k in range(4):
            place = lane + (k + 2) - cells
            steps.append((place >= width, (place + within) & (width - 1), weights[k]))
        plans.append((near, far, steps))

    def zonal_field(f):
        for l in range(levels):
            near, far, steps = plans[l]
            first = second = ring[0, f, l]
            for s in range(1, sectors):
                block = ring[s, f, l]
                first = jnp.where(near == s, block, first)
                second = jnp.where(far == s, block, second)
            total = None
            for beyond, index, weight in steps:
                value = jnp.where(beyond, take_lanes(second, index), take_lanes(first, index))
                total = weight * value if total is None else total + weight * value
            zmain[f * levels + l, own] = total
            picked = take_lanes(total, edge)
            at = f * levels + l
            if at == 0:
                zmain[both, own] = picked
            else:
                zmain[both, own] = jnp.where(group == at, picked, zmain[both, own])

    def pass_on(f):
        for d, source in enumerate(sources):
            across[f, d].wait_recv()
            relay[f, d] = remote(
                ring.at[source, f], ring.at[source, f], p_send.at[d, f], p_recv.at[d, f], la, partner
            )
            relay[f, d].start()

    zonal = []
    pass_on(0)
    for f in range(fields):
        if f + 1 < fields:
            pass_on(f + 1)
        beside[f].wait_recv()
        for d in range(halves - 1):
            relay[f, d].wait_recv()
        zonal_field(f)
        if f + 1 == fields:
            last = neighbours(zmain, zwest, zeast, both, 1, z_send, z_recv)
            for copy, goes, _ in last:
                guarded(goes, copy.start)
        pair = pl.ds(8 + 2 * f, 2)
        rowset = straight(zmain, pl.ds(f * levels, levels), z_send.at[pair], z_recv.at[pair])
        for copy, goes, _ in rowset:
            guarded(goes, copy.start)
        zonal += rowset

    for copy, _, comes in params:
        guarded(comes, copy.wait_recv)
    tall = rows + HALO
    begin = HALO // 2
    body = pl.ds(begin, tall)
    wide = lax.broadcasted_iota(jnp.int32, (tall, width), 1)
    spot = wide & (2 * HALO - 1)
    line = lax.broadcasted_iota(jnp.int32, (tall, width), 0) + (la * rows - HALO // 2)
    inside = jnp.logical_and(line >= 0, line < bands * rows)

    def coefficients(cells, frac, coupling):
        inverse = jnp.where(inside, 1.0 / (1.0 + 4.0 * coupling), 0.0)
        linked = jnp.where(inside, coupling * inverse, 0.0)
        parts = [jnp.where(inside, part, 0.0) for part in merid_parts(cells, frac)]
        return parts, linked, inverse

    def joined(left, middle, right):
        return jnp.where(spot < HALO // 2, left, jnp.where(spot >= 3 * HALO // 2, right, middle))

    level_terms = [
        coefficients(pmain[l, body], pmain[2 + l, body], pmain[4 + l, body]) for l in range(levels)
    ]
    edges = joined(pwest[0, body], pmain[6, body], peast[0, body])
    pair = wide & (4 * HALO - 1)
    strip_terms = coefficients(*[take_lanes(edges, pair + 4 * HALO * c) for c in range(3)])

    for copy, _, comes in zonal:
        guarded(comes, copy.wait_recv)
    origins = []
    for at_field in range(both):
        source = None
        for part, offset in zip(level_terms[at_field % levels][0], range(-2, 4)):
            term = part * zmain[at_field, pl.ds(begin + offset, tall)]
            source = term if source is None else source + term
        origins.append(source)

    for copy, _, comes in last:
        guarded(comes, copy.wait_recv)

    def up_down(value):
        return pltpu.roll(value, 1, 0) + pltpu.roll(value, tall - 1, 0)

    parts, linked, inverse = strip_terms
    source = None
    for part, offset in zip(parts, range(-2, 4)):
        at = pl.ds(begin + offset, tall)
        term = part * joined(zwest[0, at], zmain[both, at], zeast[0, at])
        source = term if source is None else source + term
    scaled = source * inverse
    strips = [source]
    for sweep in range(SWEEPS - 1):
        phi = strips[-1]
        around = up_down(phi) + pltpu.roll(phi, 1, 1) + pltpu.roll(phi, width - 1, 1)
        strips.append(scaled + linked * around)

    first_lane, last_lane = wide == 0, wide == width - 1
    for at_field in range(both):
        _, linked, inverse = level_terms[at_field % levels]
        source = origins[at_field]
        scaled = source * inverse
        ends = jnp.where(first_lane, HALO // 2 - 1, 3 * HALO // 2) + at_field * 2 * HALO
        phi = source
        for sweep in range(SWEEPS):
            beyond = take_lanes(strips[sweep], ends)
            before = jnp.where(first_lane, beyond, pltpu.roll(phi, 1, 1))
            after = jnp.where(last_lane, beyond, pltpu.roll(phi, width - 1, 1))
            phi = scaled + linked * (up_down(phi) + before + after)
        out[at_field // levels, at_field % levels] = phi[begin : begin + rows]

    for copy, goes, _ in params + zonal + last:
        guarded(goes, copy.wait_send)
    for f in range(fields):
        beside[f].wait_send()
        for d in range(halves - 1):
            across[f, d].wait_send()
            relay[f, d].wait_send()


def body(*args, bands, sectors):
    state = args[0]
    fields, levels, rows, width = state.shape
    both, halves = fields * levels, sectors // 2
    tall = rows + 2 * HALO
    f32 = jnp.float32
    spec = pl.BlockSpec(memory_space=pltpu.VMEM)
    pairs = pltpu.SemaphoreType.DMA((halves, fields))
    ten = pltpu.SemaphoreType.DMA((10,))
    many = pltpu.SemaphoreType.DMA((8 + 2 * fields,))
    hbm = pl.BlockSpec(memory_space=pltpu.HBM)
    small = (levels, rows, width)
    return pl.pallas_call(
        functools.partial(kernel, bands, sectors),
        out_shape=jax.ShapeDtypeStruct(state.shape, f32),
        in_specs=[hbm] * 7,
        out_specs=spec,
        scratch_shapes=[
            pltpu.VMEM((sectors,) + state.shape, f32),
            pltpu.VMEM((both + 1, tall, width), f32),
            pltpu.VMEM((1, tall, width), f32),
            pltpu.VMEM((1, tall, width), f32),
            pltpu.VMEM((7, tall, width), f32),
            pltpu.VMEM((1, tall, width), f32),
            pltpu.VMEM((1, tall, width), f32),
            pltpu.VMEM((levels, rows), jnp.int32),
            pltpu.VMEM(small, jnp.int32),
            pltpu.VMEM(small, f32),
            pltpu.VMEM(small, jnp.int32),
            pltpu.SemaphoreType.DMA((7,)),
            pairs, pairs, pairs, pairs, ten, ten, many, many,
        ],
        compiler_params=pltpu.CompilerParams(
            collective_id=0, has_side_effects=True, vmem_limit_bytes=24 * 2**20
        ),
    )(*[pltpu.with_memory_space_constraint(x, pltpu.HBM) for x in args])


def solution(mesh):
    in_specs = (
        P(None, None, "lat", "lon"),
        P(None, "lat"),
        P(None, "lat", "lon"),
        P(None, "lat", "lon"),
        P(None, "lat", "lon"),
        P(None, "lat", "lon"),
        P(None, "lat", "lon"),
    )
    out_specs = P(None, None, "lat", "lon")
    run = functools.partial(body, bands=mesh.shape["lat"], sectors=mesh.shape["lon"])
    return jax.shard_map(run, mesh=mesh, in_specs=in_specs, out_specs=out_specs, check_vma=False)
```

```python
import functools

import jax
import jax.numpy as jnp
from jax import lax
from jax.experimental import pallas as pl
from jax.experimental.pallas import tpu as pltpu
from jax.sharding import PartitionSpec as P

SWEEPS = 4
HALO = 8
MESH = pl.DeviceIdType.MESH


def cubic_weights(frac):
    return (
        -frac * (frac - 1.0) * (frac - 2.0) / 6.0,
        (frac + 1.0) * (frac - 1.0) * (frac - 2.0) / 2.0,
        -(frac + 1.0) * frac * (frac - 2.0) / 2.0,
        (frac + 1.0) * frac * (frac - 1.0) / 6.0,
    )


def take_lanes(value, index):
    return jnp.take_along_axis(value, index, axis=1, mode="promise_in_bounds")


def merid_parts(cells, frac):
    w = cubic_weights(frac)
    parts = []
    for offset in range(-2, 4):
        total = jnp.zeros_like(frac)
        for k in range(4):
            cell = k - 1 - offset
            if -1 <= cell <= 1:
                total = jnp.where(cells == float(cell), w[k], total)
        parts.append(total)
    return parts


def kernel(
    bands, sectors, state, shift_in, zcells_in, zfrac_in, mcells_in, mfrac, coup, out,
    ring, zmain, zwest, zeast, pmain, pwest, peast, shift, zcells, zfrac, mcells, loaded,
    y_send, y_recv, p_send, p_recv, h_send, h_recv, z_send, z_recv,
):
    fields, levels, rows, width = state.shape
    both = fields * levels
    halves = sectors // 2
    circle = sectors * width
    la, lo = lax.axis_index("lat"), lax.axis_index("lon")
    half = lo // 2
    core = lo - 2 * half
    partner = lo + 1 - 2 * core
    east = lax.rem(lo + 1, sectors)
    west = lax.rem(lo + sectors - 1, sectors)
    has_north, has_south = la > 0, la < bands - 1
    own = pl.ds(HALO, rows)

    barrier = pltpu.get_barrier_semaphore()

    def greet(to_la, to_lo):
        pl.semaphore_signal(barrier, inc=1, device_id=(to_la, to_lo), device_id_type=MESH)

    greet(la, east)
    greet(la, west)
    others = [2 * lax.rem(half + d, halves) + core for d in range(1, halves)]
    sources = [2 * lax.rem(half + halves - d, halves) + core for d in range(1, halves)]
    for other in others:
        greet(la, other)

    @pl.when(has_north)
    def _():
        for to_lo in (lo, east, west):
            greet(la - 1, to_lo)

    @pl.when(has_south)
    def _():
        for to_lo in (lo, east, west):
            greet(la + 1, to_lo)

    loads = [
        pltpu.make_async_copy(src, dst, loaded.at[i])
        for i, (src, dst) in enumerate((
            (state, ring.at[lo]),
            (mcells_in, mcells),
            (mfrac, pmain.at[pl.ds(levels, levels), own]),
            (coup, pmain.at[pl.ds(2 * levels, levels), own]),
            (shift_in, shift),
            (zcells_in, zcells),
            (zfrac_in, zfrac),
        ))
    ]
    for load in loads:
        load.start()

    for condition, begin in ((la == 0, 0), (la == bands - 1, rows + HALO)):
        @pl.when(condition)
        def _(begin=begin):
            for ref in (zmain, zwest, zeast):
                ref[:, pl.ds(begin, HALO), :] = jnp.zeros((ref.shape[0], HALO, width), jnp.float32)

    loads[0].wait()
    outer = jnp.logical_or(la == 0, la == bands - 1)

    @pl.when(outer)
    def _():
        pl.semaphore_wait(barrier, 1 + halves + 3)

    @pl.when(jnp.logical_not(outer))
    def _():
        pl.semaphore_wait(barrier, 1 + halves + 6)

    def remote(src, dst, send, recv, to_la, to_lo):
        return pltpu.make_async_remote_copy(
            src_ref=src, dst_ref=dst, send_sem=send, recv_sem=recv,
            device_id=(to_la, to_lo), device_id_type=MESH,
        )

    across, beside, relay = {}, {}, {}
    for f in range(fields):
        for d, other in enumerate(others):
            across[f, d] = remote(
                ring.at[lo, f], ring.at[lo, f], y_send.at[d, f], y_recv.at[d, f], la, other
            )
            across[f, d].start()
    for f in range(fields):
        beside[f] = remote(
            ring.at[lo, f], ring.at[lo, f], p_send.at[halves - 1, f], p_recv.at[halves - 1, f], la, partner
        )
        beside[f].start()

    def neighbours(main, to_west, to_east, first, count, send, recv):
        top, bottom = pl.ds(HALO, HALO), pl.ds(rows, HALO)
        before, after = pl.ds(0, HALO), pl.ds(rows + HALO, HALO)
        strip = pl.ds(first, count)
        none = None
        plan = [
            (main.at[strip, top], main.at[strip, after], la - 1, lo, has_north, has_south),
            (main.at[strip, bottom], main.at[strip, before], la + 1, lo, has_south, has_north),
            (main.at[strip, own], to_west.at[:, own], la, east, none, none),
            (main.at[strip, own], to_east.at[:, own], la, west, none, none),
            (main.at[strip, top], to_west.at[:, after], la - 1, east, has_north, has_south),
            (main.at[strip, top], to_east.at[:, after], la - 1, west, has_north, has_south),
            (main.at[strip, bottom], to_west.at[:, before], la + 1, east, has_south, has_north),
            (main.at[strip, bottom], to_east.at[:, before], la + 1, west, has_south, has_north),
        ]
        return [
            (remote(src, dst, send.at[i], recv.at[i], to_la, to_lo), goes, comes)
            for i, (src, dst, to_la, to_lo, goes, comes) in enumerate(plan)
        ]

    def straight(main, part, send, recv):
        top, bottom = pl.ds(HALO, HALO), pl.ds(rows, HALO)
        before, after = pl.ds(0, HALO), pl.ds(rows + HALO, HALO)
        return [
            (remote(main.at[part, top], main.at[part, after], send.at[0], recv.at[0], la - 1, lo),
             has_north, has_south),
            (remote(main.at[part, bottom], main.at[part, before], send.at[1], recv.at[1], la + 1, lo),
             has_south, has_north),
        ]

    def guarded(condition, action):
        if condition is None:
            action()
        else:
            pl.when(condition)(action)

    lane = lax.broadcasted_iota(jnp.int32, (rows, width), 1)
    group = lane // (2 * HALO)
    edge = ((lane & (HALO - 1)) + width - HALO // 2) & (width - 1)
    for load in loads[1:4]:
        load.wait()
    for l in range(levels):
        pmain[l, own] = mcells[l].astype(jnp.float32)
    for at in range(3):
        low, high = pmain[2 * at, own], pmain[2 * at + 1, own]
        picked = jnp.where((group & 1) == 0, take_lanes(low, edge), take_lanes(high, edge))
        packed = picked if at == 0 else jnp.where((group // 2) == at, picked, packed)
    pmain[6, own] = packed

    params = straight(pmain, pl.ds(0, 6), h_send.at[pl.ds(8, 2)], h_recv.at[pl.ds(8, 2)])
    params += neighbours(pmain, pwest, peast, 6, 1, h_send, h_recv)

    for load in loads[4:]:
        load.wait()
    square = (rows, rows)
    diagonal = lax.broadcasted_iota(jnp.int32, square, 0) == lax.broadcasted_iota(jnp.int32, square, 1)
    plans = []
    for l in range(levels):
        line = jnp.broadcast_to(shift[pl.ds(l, 1), :].astype(jnp.float32), square)
        moved = jnp.sum(jnp.where(diagonal, line, 0.0), axis=1, keepdims=True).astype(jnp.int32)
        base = lo * width - 3 - jnp.broadcast_to(moved, (rows, width))
        base = jnp.where(base < 0, base + circle, base)
        base = jnp.where(base >= circle, base - circle, base)
        hop = lax.shift_right_logical(base, width.bit_length() - 1)
        within = base & (width - 1)
        near = hop + jnp.where(lane < within, 1, 0)
        near = jnp.where(near >= sectors, near - sectors, near)
        far = near + 1
        far = jnp.where(far >= sectors, far - sectors, far)
        weights = cubic_weights(zfrac[l])
        cells = zcells[l]
        steps = []
        for k in range(4):
            place = lane + (k + 2) - cells
            steps.append((place >= width, (place + within) & (width - 1), weights[k]))
        plans.append((near, far, steps))

    def zonal_field(f):
        for l in range(levels):
            near, far, steps = plans[l]
            first = second = ring[0, f, l]
            for s in range(1, sectors):
                block = ring[s, f, l]
                first = jnp.where(near == s, block, first)
                second = jnp.where(far == s, block, second)
            total = None
            for beyond, index, weight in steps:
                value = jnp.where(beyond, take_lanes(second, index), take_lanes(first, index))
                total = weight * value if total is None else total + weight * value
            zmain[f * levels + l, own] = total
            picked = take_lanes(total, edge)
            at = f * levels + l
            if at == 0:
                zmain[both, own] = picked
            else:
                zmain[both, own] = jnp.where(group == at, picked, zmain[both, own])

    def pass_on(f):
        for d, source in enumerate(sources):
            across[f, d].wait_recv()
            relay[f, d] = remote(
                ring.at[source, f], ring.at[source, f], p_send.at[d, f], p_recv.at[d, f], la, partner
            )
            relay[f, d].start()

    zonal = []
    pass_on(0)
    for f in range(fields):
        if f + 1 < fields:
            pass_on(f + 1)
        if f + 2 == fields:
            for copy, goes, _ in params:
                guarded(goes, copy.start)
        beside[f].wait_recv()
        for d in range(halves - 1):
            relay[f, d].wait_recv()
        zonal_field(f)
        if f + 1 == fields:
            last = neighbours(zmain, zwest, zeast, both, 1, z_send, z_recv)
            for copy, goes, _ in last:
                guarded(goes, copy.start)
            zonal += last
        pair = pl.ds(8 + 2 * f, 2)
        rowset = straight(zmain, pl.ds(f * levels, levels), z_send.at[pair], z_recv.at[pair])
        for copy, goes, _ in rowset:
            guarded(goes, copy.start)
        zonal += rowset

    for copy, _, comes in params:
        guarded(comes, copy.wait_recv)
    tall = rows + HALO
    begin = HALO // 2
    body = pl.ds(begin, tall)
    wide = lax.broadcasted_iota(jnp.int32, (tall, width), 1)
    spot = wide & (2 * HALO - 1)
    line = lax.broadcasted_iota(jnp.int32, (tall, width), 0) + (la * rows - HALO // 2)
    inside = jnp.logical_and(line >= 0, line < bands * rows)

    def coefficients(cells, frac, coupling):
        inverse = jnp.where(inside, 1.0 / (1.0 + 4.0 * coupling), 0.0)
        linked = jnp.where(inside, coupling * inverse, 0.0)
        parts = [jnp.where(inside, part, 0.0) for part in merid_parts(cells, frac)]
        return parts, linked, inverse

    def joined(left, middle, right):
        return jnp.where(spot < HALO // 2, left, jnp.where(spot >= 3 * HALO // 2, right, middle))

    level_terms = [
        coefficients(pmain[l, body], pmain[2 + l, body], pmain[4 + l, body]) for l in range(levels)
    ]
    edges = joined(pwest[0, body], pmain[6, body], peast[0, body])
    pair = wide & (4 * HALO - 1)
    strip_terms = coefficients(*[take_lanes(edges, pair + 4 * HALO * c) for c in range(3)])

    for copy, _, comes in zonal:
        guarded(comes, copy.wait_recv)

    def up_down(value):
        return pltpu.roll(value, 1, 0) + pltpu.roll(value, tall - 1, 0)

    parts, linked, inverse = strip_terms
    source = None
    for part, offset in zip(parts, range(-2, 4)):
        at = pl.ds(begin + offset, tall)
        term = part * joined(zwest[0, at], zmain[both, at], zeast[0, at])
        source = term if source is None else source + term
    scaled = source * inverse
    strips = [source]
    for sweep in range(SWEEPS - 1):
        last = strips[-1]
        around = up_down(last) + pltpu.roll(last, 1, 1) + pltpu.roll(last, width - 1, 1)
        strips.append(scaled + linked * around)

    first_lane, last_lane = wide == 0, wide == width - 1
    for at_field in range(both):
        parts, linked, inverse = level_terms[at_field % levels]
        source = None
        for part, offset in zip(parts, range(-2, 4)):
            term = part * zmain[at_field, pl.ds(begin + offset, tall)]
            source = term if source is None else source + term
        scaled = source * inverse
        ends = jnp.where(first_lane, HALO // 2 - 1, 3 * HALO // 2) + at_field * 2 * HALO
        phi = source
        for sweep in range(SWEEPS):
            beyond = take_lanes(strips[sweep], ends)
            before = jnp.where(first_lane, beyond, pltpu.roll(phi, 1, 1))
            after = jnp.where(last_lane, beyond, pltpu.roll(phi, width - 1, 1))
            phi = scaled + linked * (up_down(phi) + before + after)
        out[at_field // levels, at_field % levels] = phi[begin : begin + rows]

    for copy, goes, _ in params + zonal:
        guarded(goes, copy.wait_send)
    for f in range(fields):
        beside[f].wait_send()
        for d in range(halves - 1):
            across[f, d].wait_send()
            relay[f, d].wait_send()


def body(*args, bands, sectors):
    state = args[0]
    fields, levels, rows, width = state.shape
    both, halves = fields * levels, sectors // 2
    tall = rows + 2 * HALO
    f32 = jnp.float32
    spec = pl.BlockSpec(memory_space=pltpu.VMEM)
    pairs = pltpu.SemaphoreType.DMA((halves, fields))
    ten = pltpu.SemaphoreType.DMA((10,))
    many = pltpu.SemaphoreType.DMA((8 + 2 * fields,))
    hbm = pl.BlockSpec(memory_space=pltpu.HBM)
    small = (levels, rows, width)
    return pl.pallas_call(
        functools.partial(kernel, bands, sectors),
        out_shape=jax.ShapeDtypeStruct(state.shape, f32),
        in_specs=[hbm] * 7,
        out_specs=spec,
        scratch_shapes=[
            pltpu.VMEM((sectors,) + state.shape, f32),
            pltpu.VMEM((both + 1, tall, width), f32),
            pltpu.VMEM((1, tall, width), f32),
            pltpu.VMEM((1, tall, width), f32),
            pltpu.VMEM((7, tall, width), f32),
            pltpu.VMEM((1, tall, width), f32),
            pltpu.VMEM((1, tall, width), f32),
            pltpu.VMEM((levels, rows), jnp.int32),
            pltpu.VMEM(small, jnp.int32),
            pltpu.VMEM(small, f32),
            pltpu.VMEM(small, jnp.int32),
            pltpu.SemaphoreType.DMA((7,)),
            pairs, pairs, pairs, pairs, ten, ten, many, many,
        ],
        compiler_params=pltpu.CompilerParams(
            collective_id=0, has_side_effects=True, vmem_limit_bytes=24 * 2**20
        ),
    )(*[pltpu.with_memory_space_constraint(x, pltpu.HBM) for x in args])


def solution(mesh):
    in_specs = (
        P(None, None, "lat", "lon"),
        P(None, "lat"),
        P(None, "lat", "lon"),
        P(None, "lat", "lon"),
        P(None, "lat", "lon"),
        P(None, "lat", "lon"),
        P(None, "lat", "lon"),
    )
    out_specs = P(None, None, "lat", "lon")
    run = functools.partial(body, bands=mesh.shape["lat"], sectors=mesh.shape["lon"])
    return jax.shard_map(run, mesh=mesh, in_specs=in_specs, out_specs=out_specs, check_vma=False)
```
